32 devices in a mesh: grp: 4 (over y, core), dev: 8 (over z, x).
Axes of the slice: x: 2, y: 2, z: 4, core: 2. Of those that a mesh axis runs over, the one named last changes fastest.
Arguments:
- video: float32 [64, 48, 1024], P(('grp', 'dev')), may hold values from -6 to 6
- measured: float32 [64, 48, 1024], P(('grp', 'dev')), may hold values from -6 to 6
- multiplier_tv: float32 [3, 64, 48, 1024], P(None, ('grp', 'dev')), may hold values from -3 to 3
- multiplier_fit: float32 [64, 48, 1024], P(('grp', 'dev')), may hold values from -6 to 6
- counts: int32 [64, 48], P(('grp', 'dev')), may hold values from 64 to 448
- ranking: int32 [1024], replicated, may hold values from 0 to 1023, each once
Outputs:
- video_next: float32 [64, 48, 1024], P(('grp', 'dev'))
- tv_next: float32 [3, 64, 48, 1024], P(None, ('grp', 'dev'))
- fit_next: float32 [64, 48, 1024], P(('grp', 'dev'))
The draws below stay inside these ranges and needn't reach their ends.
All inputs are finite; a program needn't handle non-finite values.
Results may differ from the reference program's by a relative error of at most 0.00005.
Values sent between devices are 32-bit elements; how exact they have to be, the bound alone decides.
A program may use at most 64 MiB of HBM per device.

```python
import jax
import jax.numpy as jnp
from jax import lax

W = 1024
R = 48
NT = 64


def touch_ends(values, key, low, high):
    longest = values.shape.index(max(values.shape))
    spots = []
    for shift in (0, 1):
        where = [jax.random.randint(jax.random.fold_in(key, axis), (), 0, length) for axis, length in enumerate(values.shape)]
        where[longest] = (where[longest] + shift) % values.shape[longest]
        spots.append(tuple(where))
    return values.at[spots[0]].set(low).at[spots[1]].set(high)


def block_scale(own_key, extent, cuts, least, largest):
    factor_of = 1.0
    for position, shards_of in cuts:
        heights = jax.random.uniform(jax.random.fold_in(jax.random.fold_in(own_key, 6), position), (shards_of,), jnp.float32, least / len(cuts), largest / len(cuts))
        factor_of = factor_of * jnp.repeat(jnp.exp(heights), extent[position] // shards_of).reshape((-1,) + (1,) * (len(extent) - 1 - position))
    return factor_of


def normal_values(key, shape, deviation, bound, shards=(), kind=jnp.bfloat16):
    level = block_scale(key, shape, shards, -0.22, 0.18) if shards else 1.0
    array = jax.random.normal(key, shape, jnp.float32) * deviation * level
    return jnp.minimum(jnp.maximum(array, -bound), bound).astype(kind)


def setup_inputs(seed: int = 0) -> dict:
    splits = jax.random.split(jax.random.key(seed), 7)
    return {
        "video": normal_values(splits[0], (NT, R, W), 1.0, 6.0, ((0, 32),), jnp.float32),
        "measured": normal_values(splits[1], (NT, R, W), 1.0, 6.0, ((0, 32),), jnp.float32),
        "multiplier_tv": normal_values(splits[2], (3, NT, R, W), 0.5, 3.0, ((1, 32),), jnp.float32),
        "multiplier_fit": normal_values(splits[3], (NT, R, W), 1.0, 6.0, ((0, 32),), jnp.float32),
        "counts": touch_ends(jax.random.randint(splits[4], (NT, R), W // 16, 7 * W // 16 + 1), jax.random.fold_in(splits[4], 1), W // 16, (7 * W // 16 + 1) - 1).astype(jnp.int32),
        "ranking": jax.random.permutation(splits[5], W).astype(jnp.int32),
    }


penalty_tv = 0.5
penalty_fit = 1.0
step_size = 0.2

def sign_table(size_n):
    left = lax.broadcasted_iota(jnp.int32, (size_n, size_n), 0)
    right = lax.broadcasted_iota(jnp.int32, (size_n, size_n), 1)
    common = jnp.bitwise_and(left, right)
    total = jnp.zeros((size_n, size_n), jnp.int32)
    for bit_index in range(max(size_n.bit_length(), 1)):
        total = total + jnp.bitwise_and(jnp.right_shift(common, bit_index), 1)
    return (1 - 2 * jnp.bitwise_and(total, 1)).astype(jnp.float32)

def transform(field):
    frames = field.shape[0]
    columns = field.shape[2]
    table_w = sign_table(columns)
    table_t = sign_table(frames)
    mixed = jnp.dot(field.reshape(-1, columns), table_w, precision=lax.Precision.HIGHEST)
    mixed = jnp.dot(table_t, mixed.reshape(frames, -1), precision=lax.Precision.HIGHEST)
    return mixed.reshape(field.shape) * (1.0 / (frames * columns) ** 0.5)

def gradient(field):
    return jnp.stack([jnp.roll(field, -1, 0) - field, jnp.roll(field, -1, 1) - field, jnp.roll(field, -1, 2) - field])

def adjoint_tv(tension):
    return jnp.roll(tension[0], 1, 0) - tension[0] + jnp.roll(tension[1], 1, 1) - tension[1] + jnp.roll(tension[2], 1, 2) - tension[2]

def reference(video, measured, multiplier_tv, multiplier_fit, counts, ranking):
    mask = (ranking[None, None, :] < counts[:, :, None]).astype(jnp.float32)
    slopes = gradient(video)
    shifted = slopes - multiplier_tv / penalty_tv
    length = jnp.sqrt(lax.optimization_barrier(jnp.sum(shifted * shifted, axis=0)))
    shrunk = shifted * (jnp.maximum(length - 1.0 / penalty_tv, 0.0) / jnp.maximum(length, 1.0 / penalty_tv))
    tension = penalty_tv * (slopes - shrunk) - multiplier_tv
    weighted = mask * (penalty_fit * (transform(video) - measured) - multiplier_fit)
    descent = adjoint_tv(tension) + transform(weighted)
    video_next = video - step_size * descent
    tv_next = multiplier_tv - penalty_tv * (gradient(video_next) - shrunk)
    fit_next = multiplier_fit - penalty_fit * mask * (transform(video_next) - measured)
    return (video_next, tv_next, fit_next)
```

```python
import functools
import math

import jax
import jax.numpy as jnp
from jax import lax
from jax.experimental import pallas as pl
from jax.experimental.pallas import tpu as pltpu
from jax.sharding import PartitionSpec as P

penalty_tv = 0.5
penalty_fit = 1.0
step_size = 0.2


def swapped(value, axis, stride):
    mask = 2**stride
    pairs = [(source, source ^ mask) for source in range(lax.axis_size(axis))]
    return lax.ppermute(value, axis, pairs)


def passed_along(value, axis, steps):
    count = lax.axis_size(axis)
    pairs = [(source, (source + steps) % count) for source in range(count)]
    return lax.ppermute(value, axis, pairs)


def sign_table(size_n):
    left = lax.broadcasted_iota(jnp.int32, (size_n, size_n), 0)
    right = lax.broadcasted_iota(jnp.int32, (size_n, size_n), 1)
    common = jnp.bitwise_and(left, right)
    total = jnp.zeros((size_n, size_n), jnp.int32)
    for bit_index in range(max(size_n.bit_length(), 1)):
        total = total + jnp.bitwise_and(jnp.right_shift(common, bit_index), 1)
    return (1 - 2 * jnp.bitwise_and(total, 1)).astype(jnp.float32)


def pair_steps(field, axis_kind):
    count = lax.axis_size("dev") if axis_kind == "dev" else lax.axis_size("grp")
    for bit_index in range(count.bit_length() - 1):
        if axis_kind == "dev":
            partner = swapped(field, "dev", bit_index)
            my_bit = jnp.bitwise_and(jnp.right_shift(lax.axis_index("dev"), bit_index), 1)
        else:
            partner = swapped(field, "grp", bit_index)
            my_bit = jnp.bitwise_and(jnp.right_shift(lax.axis_index("grp"), bit_index), 1)
        field = jnp.where(my_bit == 1, partner - field, field + partner)
    return field


def time_local(field, table_t):
    return jnp.einsum("st,trc->src", table_t, field, precision=lax.Precision.HIGHEST)


def transform(field):
    frames, rows, columns = field.shape
    dev_count = lax.axis_size("dev")
    grp_count = lax.axis_size("grp")
    total_frames = frames * dev_count * grp_count
    scale = 1.0 / math.sqrt(total_frames * columns)
    table_w = sign_table(columns)
    mixed = jnp.dot(field.reshape(-1, columns), table_w, precision=lax.Precision.HIGHEST).reshape(
        field.shape
    )
    mixed = time_local(mixed, sign_table(frames))
    mixed = pair_steps(mixed, "dev")
    mixed = pair_steps(mixed, "grp")
    return mixed * scale


def gradient(field):
    after = passed_along(field[:1], ("grp", "dev"), -1)
    extended = jnp.concatenate([field[1:], after], axis=0)
    return jnp.stack(
        [extended - field, jnp.roll(field, -1, 1) - field, jnp.roll(field, -1, 2) - field]
    )


def adjoint_tv(tension):
    before = passed_along(tension[0, -1:], ("grp", "dev"), 1)
    previous = jnp.concatenate([before, tension[0, :-1]], axis=0)
    return (
        previous
        - tension[0]
        + jnp.roll(tension[1], 1, 1)
        - tension[1]
        + jnp.roll(tension[2], 1, 2)
        - tension[2]
    )


def body(video, measured, multiplier_tv, multiplier_fit, counts, ranking):
    mask = (ranking[None, None, :] < counts[:, :, None]).astype(jnp.float32)
    slopes = gradient(video)
    shifted = slopes - multiplier_tv / penalty_tv
    length = jnp.sqrt(jnp.sum(shifted * shifted, axis=0))
    shrunk = shifted * (
        jnp.maximum(length - 1.0 / penalty_tv, 0.0) / jnp.maximum(length, 1.0 / penalty_tv)
    )
    tension = penalty_tv * (slopes - shrunk) - multiplier_tv
    weighted = mask * (penalty_fit * (transform(video) - measured) - multiplier_fit)
    descent = adjoint_tv(tension) + transform(weighted)
    video_next = video - step_size * descent
    tv_next = multiplier_tv - penalty_tv * (gradient(video_next) - shrunk)
    fit_next = multiplier_fit - penalty_fit * mask * (transform(video_next) - measured)
    return (video_next, tv_next, fit_next)


LANES = 128
USED = 112
GROUPS = 4
ROW_GROUPS = 8
CHUNKS = GROUPS * ROW_GROUPS
MESH_ID = pl.DeviceIdType.MESH


def walsh(value):
    size = value.shape[0]
    tail = value.shape[1:]
    half = 1
    while half < size:
        pairs = value.reshape((size // (2 * half), 2, half) + tail)
        low, high = pairs[:, 0:1], pairs[:, 1:2]
        value = jnp.concatenate([low + high, low - high], axis=1).reshape((size,) + tail)
        half *= 2
    return value


def halves(value):
    high = value.astype(jnp.bfloat16)
    low = (value - high.astype(jnp.float32)).astype(jnp.bfloat16)
    return jnp.concatenate([high, low], axis=0)


def times_transposed(value, table):
    out = lax.dot_general(
        halves(value), table, (((1,), (1,)), ((), ())), preferred_element_type=jnp.float32
    )
    return out[: value.shape[0]] + out[value.shape[0] :]


def times(value, table):
    out = jnp.dot(halves(value), table, preferred_element_type=jnp.float32)
    return out[: value.shape[0]] + out[value.shape[0] :]


def kernel(
    dev_count, count, scale,
    video, measured, mult_tv, mult_fit, counts, ranking,
    video_next, tv_next, fit_next,
    select, signs, mat, mat3, part, tens,
    s_v, s_q, s_u, s_t, s_e,
    r_v, r_q, r_u, r_t, r_e,
    h_v, h_t, h_u, weighted, known, keep,
    send_sem, recv_sem, halo_send, halo_recv,
):
    rows, columns = video.shape[1], video.shape[2]
    span = rows // ROW_GROUPS
    me = lax.axis_index("grp") * dev_count + lax.axis_index("dev")
    after = lax.rem(me + 1, count)
    before = lax.rem(me + count - 1, count)

    def coords(index):
        return (index // dev_count, lax.rem(index, dev_count))

    barrier = pltpu.get_barrier_semaphore()

    def greet(step, carry):
        other = lax.rem(me + step, count)
        pl.semaphore_signal(barrier, inc=1, device_id=coords(other), device_id_type=MESH_ID)
        return carry

    lax.fori_loop(1, count, greet, 0)

    def halo(slot, source, target, other):
        copy = pltpu.make_async_remote_copy(
            src_ref=source, dst_ref=target, send_sem=halo_send.at[slot],
            recv_sem=halo_recv.at[slot], device_id=coords(other), device_id_type=MESH_ID,
        )
        copy.start()
        return copy

    def spread(slot, source, target):
        def step_to(step, carry):
            other = lax.rem(me + step, count)
            pltpu.make_async_remote_copy(
                src_ref=source(other), dst_ref=target.at[me], send_sem=send_sem.at[slot],
                recv_sem=recv_sem.at[slot], device_id=coords(other), device_id_type=MESH_ID,
            ).start()
            return carry

        lax.fori_loop(1, count, step_to, 0)

    def arrived(slot, target):
        held = target.at[pl.ds(0, count - 1)]
        pltpu.make_async_copy(held, held, recv_sem.at[slot]).wait()

    def sent(slot, target):
        held = target.at[pl.ds(0, count - 1)]
        pltpu.make_async_copy(held, held, send_sem.at[slot]).wait()

    def cut(value, target):
        mat[...] = value
        for chunk in range(CHUNKS):
            row, lane = chunk // GROUPS * span, chunk % GROUPS * LANES
            for frame in range(2):
                start = frame * rows + row
                target[chunk, frame] = mat[start : start + span, lane : lane + LANES]

    def paste(source, target, frames):
        for chunk in range(CHUNKS):
            row, lane = chunk // GROUPS * span, chunk % GROUPS * LANES
            for frame in range(frames):
                start = frame * rows + row
                target[start : start + span, lane : lane + LANES] = source[chunk, frame]

    wide = GROUPS * LANES
    place = lax.broadcasted_iota(jnp.int32, (wide, LANES), 0)
    inner = lax.rem(place, LANES)
    rank = jnp.where(inner < USED, place // LANES * USED + inner, -1)
    lane_index = lax.broadcasted_iota(jnp.int32, (wide, LANES), 1)
    picked = jnp.zeros((wide, LANES), jnp.int32)
    for tile in range(columns // LANES):
        cols = slice(tile * LANES, (tile + 1) * LANES)
        hit = ranking[:, cols] == rank
        select[:, cols] = jnp.where(hit, 1.0, 0.0).astype(jnp.bfloat16)
        picked = picked + jnp.where(hit, lane_index + tile * LANES, 0)
    column = jnp.sum(picked.astype(jnp.float32), axis=1, keepdims=True).astype(jnp.int32)
    common = jnp.bitwise_and(column, lane_index)
    for shift in (4, 2, 1):
        common = jnp.bitwise_xor(common, jnp.right_shift(common, shift))
    low_sign = (1 - 2 * jnp.bitwise_and(common, 1)).astype(jnp.float32)
    for tile in range(columns // LANES):
        high = jnp.bitwise_and(jnp.right_shift(column, LANES.bit_length() - 1), tile)
        for shift in (4, 2, 1):
            high = jnp.bitwise_xor(high, jnp.right_shift(high, shift))
        sign = (1 - 2 * jnp.bitwise_and(high, 1)).astype(jnp.float32)
        signs[:, tile * LANES : (tile + 1) * LANES] = (low_sign * sign).astype(jnp.bfloat16)

    pl.semaphore_wait(barrier, count - 1)
    halo_v = halo(0, video.at[0], h_v, before)

    flat = (2 * rows, columns)
    cut(times_transposed(video[...].reshape(flat), signs[...]), s_v)
    spread(0, lambda other: s_v.at[other], r_v)
    r_v[me] = s_v[me]

    square = (rows, rows)
    diagonal = lax.broadcasted_iota(jnp.int32, square, 0) == lax.broadcasted_iota(
        jnp.int32, square, 1
    )
    kept = []
    for frame in range(2):
        line = counts[frame : frame + 1, :].astype(jnp.float32)
        kept.append(jnp.sum(jnp.where(diagonal, line, 0.0), axis=1, keepdims=True))
    kept = jnp.concatenate(kept, axis=0)
    wanted = times_transposed((measured[...] + mult_fit[...]).reshape(flat), select[...])
    spare = lax.rem(lax.broadcasted_iota(jnp.int32, wanted.shape, 1), LANES) >= USED
    cut(jnp.where(spare, kept, wanted), s_q)
    spread(1, lambda other: s_q.at[other], r_q)
    r_q[me] = s_q[me]
    mask = ranking[...].astype(jnp.float32) < kept
    known[...] = mult_fit[...].reshape(flat) + jnp.where(mask, measured[...].reshape(flat), 0.0)

    halo_v.wait()
    for frame in (1, 0):
        here = video[frame]
        ahead = h_v[...] if frame == 1 else video[1]
        slopes = (
            ahead - here,
            pltpu.roll(here, rows - 1, 0) - here,
            pltpu.roll(here, columns - 1, 1) - here,
        )
        shifted = [slopes[k] - mult_tv[k, frame] / penalty_tv for k in range(3)]
        length = jnp.sqrt(
            shifted[0] * shifted[0] + shifted[1] * shifted[1] + shifted[2] * shifted[2]
        )
        edge = 1.0 / penalty_tv
        factor = jnp.maximum(length - edge, 0.0) / jnp.maximum(length, edge)
        for k in range(3):
            shrunk = shifted[k] * factor
            tens[k, frame] = penalty_tv * (slopes[k] - shrunk) - mult_tv[k, frame]
            part[k, frame] = mult_tv[k, frame] + penalty_tv * shrunk
        if frame == 1:
            halo_t = halo(1, tens.at[0, 1], h_t, after)

    arrived(0, r_v)
    arrived(1, r_q)
    chunk_shape = (2 * count, span, LANES)
    spectrum = walsh(r_v[...].reshape(chunk_shape)) * scale
    wish = r_q[...].reshape(chunk_shape)
    lanes = lax.broadcasted_iota(jnp.int32, chunk_shape, 2)
    own_rank = (lax.rem(me, GROUPS) * USED + lanes).astype(jnp.float32)
    inside = jnp.logical_and(lanes < USED, own_rank < wish[:, :, LANES - 1 :])
    keep[...] = jnp.where(inside, 1.0, 0.0)
    fresh = jnp.where(inside, spectrum - wish, 0.0) * penalty_fit
    weighted[...] = fresh
    back = walsh(fresh) * (scale * step_size)
    s_t[: 2 * count] = back
    s_t[2 * count :] = back[:1]
    spread(2, lambda other: s_t.at[pl.ds(2 * other, 3)], r_t)
    r_t[me] = s_t[pl.ds(2 * me, 3)]

    halo_t.wait()
    for frame in range(2):
        previous = h_t[...] if frame == 0 else tens[0, 0]
        adjoint = (
            previous
            - tens[0, frame]
            + pltpu.roll(tens[1, frame], 1, 0)
            - tens[1, frame]
            + pltpu.roll(tens[2, frame], 1, 1)
            - tens[2, frame]
        )
        tens[1 + frame, 0] = video[frame] - step_size * adjoint
    halo_u = halo(2, tens.at[1, 0], h_u, before)
    stepped = jnp.concatenate([tens[1, 0], tens[2, 0]], axis=0)
    cut(times_transposed(stepped, signs[...]), s_u)
    spread(3, lambda other: s_u.at[other], r_u)
    r_u[me] = s_u[me]

    arrived(3, r_u)
    spectrum = walsh(r_u[...].reshape(chunk_shape)) * scale
    left = keep[...] * penalty_fit * (spectrum - step_size * weighted[...])
    s_e[...] = left.reshape(s_e.shape)
    spread(4, lambda other: s_e.at[other], r_e)
    r_e[me] = s_e[me]

    arrived(2, r_t)
    paste(r_t, mat3, 3)
    change = times(mat3[...], signs[...])
    halo_u.wait()
    first = tens[1, 0] - change[:rows]
    second = tens[2, 0] - change[rows : 2 * rows]
    third = h_u[...] - change[2 * rows :]
    video_next[0] = first
    video_next[1] = second
    for frame, here, ahead in ((0, first, second), (1, second, third)):
        tv_next[0, frame] = part[0, frame] - penalty_tv * (ahead - here)
        tv_next[1, frame] = part[1, frame] - penalty_tv * (pltpu.roll(here, rows - 1, 0) - here)
        tv_next[2, frame] = part[2, frame] - penalty_tv * (pltpu.roll(here, columns - 1, 1) - here)

    arrived(4, r_e)
    paste(r_e, mat, 2)
    fit_next[...] = (known[...] - times(mat[...], select[...])).reshape(fit_next.shape)

    sent(0, r_v)
    sent(1, r_q)
    sent(2, r_t)
    sent(3, r_u)
    sent(4, r_e)


def fused(dev_count, count, video, measured, mult_tv, mult_fit, counts, ranking):
    frames, rows, columns = video.shape
    span = rows // ROW_GROUPS
    wide = GROUPS * LANES
    f32 = jnp.float32
    block = pltpu.VMEM((count, frames, span, LANES), f32)
    scratch = [
        pltpu.VMEM((wide, columns), jnp.bfloat16),
        pltpu.VMEM((wide, columns), jnp.bfloat16),
        pltpu.VMEM((frames * rows, wide), f32),
        pltpu.VMEM(((frames + 1) * rows, wide), f32),
        pltpu.VMEM(mult_tv.shape, f32),
        pltpu.VMEM(mult_tv.shape, f32),
        block, block, block,
        pltpu.VMEM((frames * count + 1, span, LANES), f32),
        block,
        block, block, block,
        pltpu.VMEM((count, frames + 1, span, LANES), f32),
        block,
        pltpu.VMEM((rows, columns), f32),
        pltpu.VMEM((rows, columns), f32),
        pltpu.VMEM((rows, columns), f32),
        pltpu.VMEM((frames * count, span, LANES), f32),
        pltpu.VMEM((frames * rows, columns), f32),
        pltpu.VMEM((frames * count, span, LANES), f32),
        pltpu.SemaphoreType.DMA((5,)),
        pltpu.SemaphoreType.DMA((5,)),
        pltpu.SemaphoreType.DMA((3,)),
        pltpu.SemaphoreType.DMA((3,)),
    ]
    scale = 1.0 / math.sqrt(frames * count * columns)
    vmem = pl.BlockSpec(memory_space=pltpu.VMEM)
    return pl.pallas_call(
        functools.partial(kernel, dev_count, count, scale),
        out_shape=(
            jax.ShapeDtypeStruct(video.shape, f32),
            jax.ShapeDtypeStruct(mult_tv.shape, f32),
            jax.ShapeDtypeStruct(video.shape, f32),
        ),
        in_specs=[vmem] * 6,
        out_specs=(vmem, vmem, vmem),
        scratch_shapes=scratch,
        compiler_params=pltpu.CompilerParams(
            collective_id=0, has_side_effects=True, vmem_limit_bytes=48 * 2**20
        ),
    )(video, measured, mult_tv, mult_fit, counts, ranking.reshape(1, columns))


def solution(mesh):
    placed = (
        P(("grp", "dev"), None, None),
        P(("grp", "dev"), None, None),
        P(None, ("grp", "dev"), None, None),
        P(("grp", "dev"), None, None),
        P(("grp", "dev"), None),
        P(),
    )
    dev_count = mesh.shape["dev"]
    count = dev_count * mesh.shape["grp"]
    local = functools.partial(fused, dev_count, count) if count == CHUNKS else body
    return jax.shard_map(
        local,
        mesh=mesh,
        in_specs=placed,
        out_specs=(
            P(("grp", "dev"), None, None),
            P(None, ("grp", "dev"), None, None),
            P(("grp", "dev"), None, None),
        ),
        check_vma=False,
    )
```

```python
import functools
import math

import jax
import jax.numpy as jnp
from jax import lax
from jax.experimental import pallas as pl
from jax.experimental.pallas import tpu as pltpu
from jax.sharding import PartitionSpec as P

penalty_tv = 0.5
penalty_fit = 1.0
step_size = 0.2


def swapped(value, axis, stride):
    mask = 2**stride
    pairs = [(source, source ^ mask) for source in range(lax.axis_size(axis))]
    return lax.ppermute(value, axis, pairs)


def passed_along(value, axis, steps):
    count = lax.axis_size(axis)
    pairs = [(source, (source + steps) % count) for source in range(count)]
    return lax.ppermute(value, axis, pairs)


def sign_table(size_n):
    left = lax.broadcasted_iota(jnp.int32, (size_n, size_n), 0)
    right = lax.broadcasted_iota(jnp.int32, (size_n, size_n), 1)
    common = jnp.bitwise_and(left, right)
    total = jnp.zeros((size_n, size_n), jnp.int32)
    for bit_index in range(max(size_n.bit_length(), 1)):
        total = total + jnp.bitwise_and(jnp.right_shift(common, bit_index), 1)
    return (1 - 2 * jnp.bitwise_and(total, 1)).astype(jnp.float32)


def pair_steps(field, axis_kind):
    count = lax.axis_size("dev") if axis_kind == "dev" else lax.axis_size("grp")
    for bit_index in range(count.bit_length() - 1):
        if axis_kind == "dev":
            partner = swapped(field, "dev", bit_index)
            my_bit = jnp.bitwise_and(jnp.right_shift(lax.axis_index("dev"), bit_index), 1)
        else:
            partner = swapped(field, "grp", bit_index)
            my_bit = jnp.bitwise_and(jnp.right_shift(lax.axis_index("grp"), bit_index), 1)
        field = jnp.where(my_bit == 1, partner - field, field + partner)
    return field


def time_local(field, table_t):
    return jnp.einsum("st,trc->src", table_t, field, precision=lax.Precision.HIGHEST)


def transform(field):
    frames, rows, columns = field.shape
    dev_count = lax.axis_size("dev")
    grp_count = lax.axis_size("grp")
    total_frames = frames * dev_count * grp_count
    scale = 1.0 / math.sqrt(total_frames * columns)
    table_w = sign_table(columns)
    mixed = jnp.dot(field.reshape(-1, columns), table_w, precision=lax.Precision.HIGHEST).reshape(
        field.shape
    )
    mixed = time_local(mixed, sign_table(frames))
    mixed = pair_steps(mixed, "dev")
    mixed = pair_steps(mixed, "grp")
    return mixed * scale


def gradient(field):
    after = passed_along(field[:1], ("grp", "dev"), -1)
    extended = jnp.concatenate([field[1:], after], axis=0)
    return jnp.stack(
        [extended - field, jnp.roll(field, -1, 1) - field, jnp.roll(field, -1, 2) - field]
    )


def adjoint_tv(tension):
    before = passed_along(tension[0, -1:], ("grp", "dev"), 1)
    previous = jnp.concatenate([before, tension[0, :-1]], axis=0)
    return (
        previous
        - tension[0]
        + jnp.roll(tension[1], 1, 1)
        - tension[1]
        + jnp.roll(tension[2], 1, 2)
        - tension[2]
    )


def body(video, measured, multiplier_tv, multiplier_fit, counts, ranking):
    mask = (ranking[None, None, :] < counts[:, :, None]).astype(jnp.float32)
    slopes = gradient(video)
    shifted = slopes - multiplier_tv / penalty_tv
    length = jnp.sqrt(jnp.sum(shifted * shifted, axis=0))
    shrunk = shifted * (
        jnp.maximum(length - 1.0 / penalty_tv, 0.0) / jnp.maximum(length, 1.0 / penalty_tv)
    )
    tension = penalty_tv * (slopes - shrunk) - multiplier_tv
    weighted = mask * (penalty_fit * (transform(video) - measured) - multiplier_fit)
    descent = adjoint_tv(tension) + transform(weighted)
    video_next = video - step_size * descent
    tv_next = multiplier_tv - penalty_tv * (gradient(video_next) - shrunk)
    fit_next = multiplier_fit - penalty_fit * mask * (transform(video_next) - measured)
    return (video_next, tv_next, fit_next)


LANES = 128
USED = 112
GROUPS = 4
ROW_GROUPS = 8
CHUNKS = GROUPS * ROW_GROUPS
MESH_ID = pl.DeviceIdType.MESH


def walsh(value):
    size = value.shape[0]
    tail = value.shape[1:]
    half = 1
    while half < size:
        pairs = value.reshape((size // (2 * half), 2, half) + tail)
        low, high = pairs[:, 0:1], pairs[:, 1:2]
        value = jnp.concatenate([low + high, low - high], axis=1).reshape((size,) + tail)
        half *= 2
    return value


def halves(value):
    high = value.astype(jnp.bfloat16)
    low = (value - high.astype(jnp.float32)).astype(jnp.bfloat16)
    return jnp.concatenate([high, low], axis=0)


def times_transposed(value, table):
    out = lax.dot_general(
        halves(value), table, (((1,), (1,)), ((), ())), preferred_element_type=jnp.float32
    )
    return out[: value.shape[0]] + out[value.shape[0] :]


def times(value, table):
    out = jnp.dot(halves(value), table, preferred_element_type=jnp.float32)
    return out[: value.shape[0]] + out[value.shape[0] :]


def kernel(
    dev_count, count, scale,
    video_in, measured_in, mult_tv_in, mult_fit_in, counts_in, ranking_in,
    video_next, tv_next, fit_next,
    video, measured, mult_tv, mult_fit, counts, ranking,
    select, signs, mat, part, tens, moved,
    s_v, s_q, s_u, s_t, s_e,
    r_v, r_q, r_u, r_t, r_e,
    h_v, h_t, h_u, weighted, known, keep,
    load_sem, send_sem, recv_sem, halo_send, halo_recv,
):
    rows, columns = video.shape[1], video.shape[2]
    span = rows // ROW_GROUPS
    me = lax.axis_index("grp") * dev_count + lax.axis_index("dev")
    after = lax.rem(me + 1, count)
    before = lax.rem(me + count - 1, count)

    def coords(index):
        return (index // dev_count, lax.rem(index, dev_count))

    loads = [
        pltpu.make_async_copy(source, target, load_sem.at[slot])
        for slot, (source, target) in enumerate(
            (
                (ranking_in, ranking),
                (counts_in, counts),
                (video_in, video),
                (mult_tv_in, mult_tv),
                (measured_in, measured),
                (mult_fit_in, mult_fit),
            )
        )
    ]
    for load in loads:
        load.start()

    barrier = pltpu.get_barrier_semaphore()

    def greet(step, carry):
        other = lax.rem(me + step, count)
        pl.semaphore_signal(barrier, inc=1, device_id=coords(other), device_id_type=MESH_ID)
        return carry

    lax.fori_loop(1, count, greet, 0)

    def halo(slot, source, target, other):
        copy = pltpu.make_async_remote_copy(
            src_ref=source, dst_ref=target, send_sem=halo_send.at[slot],
            recv_sem=halo_recv.at[slot], device_id=coords(other), device_id_type=MESH_ID,
        )
        copy.start()
        return copy

    def spread(slot, source, target, frame=None):
        def step_to(step, carry):
            other = lax.rem(me + step, count)
            pltpu.make_async_remote_copy(
                src_ref=source(other),
                dst_ref=target.at[me] if frame is None else target.at[me, frame],
                send_sem=send_sem.at[slot],
                recv_sem=recv_sem.at[slot], device_id=coords(other), device_id_type=MESH_ID,
            ).start()
            return carry

        lax.fori_loop(1, count, step_to, 0)

    def arrived(slot, target, frame=None):
        held = target.at[pl.ds(0, count - 1)] if frame is None else target.at[pl.ds(0, count - 1), frame]
        pltpu.make_async_copy(held, held, recv_sem.at[slot]).wait()

    def sent(slot, target, frame=None):
        held = target.at[pl.ds(0, count - 1)] if frame is None else target.at[pl.ds(0, count - 1), frame]
        pltpu.make_async_copy(held, held, send_sem.at[slot]).wait()

    def cut_frame(value, target, frame):
        mat[:rows] = value
        for chunk in range(CHUNKS):
            row, lane = chunk // GROUPS * span, chunk % GROUPS * LANES
            target[chunk, frame] = mat[row : row + span, lane : lane + LANES]

    def cut(value, target):
        mat[...] = value
        for chunk in range(CHUNKS):
            row, lane = chunk // GROUPS * span, chunk % GROUPS * LANES
            for frame in range(2):
                start = frame * rows + row
                target[chunk, frame] = mat[start : start + span, lane : lane + LANES]

    def paste(source, target, frames):
        for chunk in range(CHUNKS):
            row, lane = chunk // GROUPS * span, chunk % GROUPS * LANES
            for frame in range(frames):
                start = frame * rows + row
                target[start : start + span, lane : lane + LANES] = source[chunk, frame]

    pl.semaphore_wait(barrier, count - 1)
    piece = rows // 2
    pieces = [pl.ds(0, piece), pl.ds(piece, piece)]
    halo_v = [
        halo(n, video_in.at[0, cut_rows], h_v.at[cut_rows], before)
        for n, cut_rows in enumerate(pieces)
    ]

    loads[0].wait()
    wide = GROUPS * LANES
    place = lax.broadcasted_iota(jnp.int32, (wide, LANES), 0)
    inner = lax.rem(place, LANES)
    rank = jnp.where(inner < USED, place // LANES * USED + inner, -1)
    lane_index = lax.broadcasted_iota(jnp.int32, (wide, LANES), 1)
    picked = jnp.zeros((wide, LANES), jnp.int32)
    for tile in range(columns // LANES):
        cols = slice(tile * LANES, (tile + 1) * LANES)
        hit = ranking[:, cols] == rank
        select[:, cols] = jnp.where(hit, 1.0, 0.0).astype(jnp.bfloat16)
        picked = picked + jnp.where(hit, lane_index + tile * LANES, 0)
    column = jnp.sum(picked.astype(jnp.float32), axis=1, keepdims=True).astype(jnp.int32)
    common = jnp.bitwise_and(column, lane_index)
    for shift in (4, 2, 1):
        common = jnp.bitwise_xor(common, jnp.right_shift(common, shift))
    low_sign = (1 - 2 * jnp.bitwise_and(common, 1)).astype(jnp.float32)
    for tile in range(columns // LANES):
        high = jnp.bitwise_and(jnp.right_shift(column, LANES.bit_length() - 1), tile)
        for shift in (4, 2, 1):
            high = jnp.bitwise_xor(high, jnp.right_shift(high, shift))
        sign = (1 - 2 * jnp.bitwise_and(high, 1)).astype(jnp.float32)
        signs[:, tile * LANES : (tile + 1) * LANES] = (low_sign * sign).astype(jnp.bfloat16)

    flat = (2 * rows, columns)
    loads[2].wait()
    cut(times_transposed(video[...].reshape(flat), signs[...]), s_v)
    spread(0, lambda other: s_v.at[other], r_v)
    r_v[me] = s_v[me]

    for load in (loads[1], loads[4], loads[5]):
        load.wait()
    square = (rows, rows)
    diagonal = lax.broadcasted_iota(jnp.int32, square, 0) == lax.broadcasted_iota(
        jnp.int32, square, 1
    )
    kept = []
    for frame in range(2):
        line = counts[frame : frame + 1, :].astype(jnp.float32)
        kept.append(jnp.sum(jnp.where(diagonal, line, 0.0), axis=1, keepdims=True))
    kept = jnp.concatenate(kept, axis=0)
    wanted = times_transposed((measured[...] + mult_fit[...]).reshape(flat), select[...])
    spare = lax.rem(lax.broadcasted_iota(jnp.int32, wanted.shape, 1), LANES) >= USED
    cut(jnp.where(spare, kept, wanted), s_q)

    loads[3].wait()

    def shrink(frame, where, ahead, down, right):
        here = video[frame, where]
        slopes = (ahead - here, down - here, right - here)
        mult = [mult_tv[k, frame, where] for k in range(3)]
        shifted = [slopes[k] - mult[k] / penalty_tv for k in range(3)]
        length = jnp.sqrt(
            shifted[0] * shifted[0] + shifted[1] * shifted[1] + shifted[2] * shifted[2]
        )
        edge = 1.0 / penalty_tv
        factor = jnp.maximum(length - edge, 0.0) / jnp.maximum(length, edge)
        for k in range(3):
            shrunk = shifted[k] * factor
            tens[k, frame, where] = penalty_tv * (slopes[k] - shrunk) - mult[k]
            part[k, frame, where] = mult[k] + penalty_tv * shrunk

    def rolled(frame):
        here = video[frame]
        return pltpu.roll(here, rows - 1, 0), pltpu.roll(here, columns - 1, 1)

    shrink(0, pl.ds(0, rows), video[1], *rolled(0))
    down, right = rolled(1)
    halo_t = []
    for n, where in enumerate(pieces):
        halo_v[n].wait()
        span_rows = slice(n * piece, (n + 1) * piece)
        shrink(1, where, h_v[where], down[span_rows], right[span_rows])
        halo_t.append(halo(2 + n, tens.at[0, 1, where], h_t.at[where], after))
    spread(1, lambda other: s_q.at[other], r_q)
    r_q[me] = s_q[me]

    def stepped(frame, previous):
        adjoint = (
            previous
            - tens[0, frame]
            + pltpu.roll(tens[1, frame], 1, 0)
            - tens[1, frame]
            + pltpu.roll(tens[2, frame], 1, 1)
            - tens[2, frame]
        )
        result = video[frame] - step_size * adjoint
        moved[frame] = result
        cut_frame(times_transposed(result, signs[...]), s_u, frame)
        spread(3 + frame, lambda other: s_u.at[other, frame], r_u, frame)
        r_u[me, frame] = s_u[me, frame]

    stepped(1, tens[0, 0])
    mask = ranking[...].astype(jnp.float32) < kept
    known[...] = mult_fit[...].reshape(flat) + jnp.where(mask, measured[...].reshape(flat), 0.0)
    halo_t[0].wait()
    halo_t[1].wait()
    stepped(0, h_t[...])

    arrived(0, r_v)
    arrived(1, r_q)
    chunk_shape = (2 * count, span, LANES)
    spectrum = walsh(r_v[...].reshape(chunk_shape)) * scale
    wish = r_q[...].reshape(chunk_shape)
    lanes = lax.broadcasted_iota(jnp.int32, chunk_shape, 2)
    own_rank = (lax.rem(me, GROUPS) * USED + lanes).astype(jnp.float32)
    inside = jnp.logical_and(lanes < USED, own_rank < wish[:, :, LANES - 1 :])
    keep[...] = jnp.where(inside, 1.0, 0.0)
    fresh = jnp.where(inside, spectrum - wish, 0.0) * penalty_fit
    weighted[...] = fresh
    back = walsh(fresh) * (scale * step_size)
    s_t[...] = back.reshape(s_t.shape)
    spread(2, lambda other: s_t.at[other], r_t)
    r_t[me] = s_t[me]

    arrived(3, r_u, 0)
    arrived(4, r_u, 1)
    spectrum = walsh(r_u[...].reshape(chunk_shape)) * scale
    left = keep[...] * penalty_fit * (spectrum - step_size * weighted[...])
    s_e[...] = left.reshape(s_e.shape)
    spread(5, lambda other: s_e.at[other], r_e)
    r_e[me] = s_e[me]

    arrived(2, r_t)
    paste(r_t, mat, 2)
    change = times(mat[...], signs[...])
    first = moved[0] - change[:rows]
    second = moved[1] - change[rows:]
    moved[0] = first
    halo_u = halo(4, moved.at[0], h_u, before)
    video_next[0] = first
    video_next[1] = second
    for frame, here in ((0, first), (1, second)):
        tv_next[1, frame] = part[1, frame] - penalty_tv * (pltpu.roll(here, rows - 1, 0) - here)
        tv_next[2, frame] = part[2, frame] - penalty_tv * (pltpu.roll(here, columns - 1, 1) - here)
    tv_next[0, 0] = part[0, 0] - penalty_tv * (second - first)
    arrived(5, r_e)
    paste(r_e, mat, 2)
    fit_next[...] = (known[...] - times(mat[...], select[...])).reshape(fit_next.shape)

    halo_u.wait()
    tv_next[0, 1] = part[0, 1] - penalty_tv * (h_u[...] - video_next[1])
    sent(0, r_v)
    sent(1, r_q)
    sent(2, r_t)
    sent(3, r_u, 0)
    sent(4, r_u, 1)
    sent(5, r_e)


def fused(dev_count, count, video, measured, mult_tv, mult_fit, counts, ranking):
    frames, rows, columns = video.shape
    span = rows // ROW_GROUPS
    wide = GROUPS * LANES
    f32 = jnp.float32
    block = pltpu.VMEM((count, frames, span, LANES), f32)
    scratch = [
        pltpu.VMEM(video.shape, f32),
        pltpu.VMEM(video.shape, f32),
        pltpu.VMEM(mult_tv.shape, f32),
        pltpu.VMEM(video.shape, f32),
        pltpu.VMEM(counts.shape, jnp.int32),
        pltpu.VMEM((1, columns), jnp.int32),
        pltpu.VMEM((wide, columns), jnp.bfloat16),
        pltpu.VMEM((wide, columns), jnp.bfloat16),
        pltpu.VMEM((frames * rows, wide), f32),
        pltpu.VMEM(mult_tv.shape, f32),
        pltpu.VMEM(mult_tv.shape, f32),
        pltpu.VMEM(video.shape, f32),
        block, block, block, block, block,
        block, block, block, block, block,
        pltpu.VMEM((rows, columns), f32),
        pltpu.VMEM((rows, columns), f32),
        pltpu.VMEM((rows, columns), f32),
        pltpu.VMEM((frames * count, span, LANES), f32),
        pltpu.VMEM((frames * rows, columns), f32),
        pltpu.VMEM((frames * count, span, LANES), f32),
        pltpu.SemaphoreType.DMA((6,)),
        pltpu.SemaphoreType.DMA((6,)),
        pltpu.SemaphoreType.DMA((6,)),
        pltpu.SemaphoreType.DMA((5,)),
        pltpu.SemaphoreType.DMA((5,)),
    ]
    scale = 1.0 / math.sqrt(frames * count * columns)
    vmem = pl.BlockSpec(memory_space=pltpu.VMEM)
    return pl.pallas_call(
        functools.partial(kernel, dev_count, count, scale),
        out_shape=(
            jax.ShapeDtypeStruct(video.shape, f32),
            jax.ShapeDtypeStruct(mult_tv.shape, f32),
            jax.ShapeDtypeStruct(video.shape, f32),
        ),
        in_specs=[pl.BlockSpec(memory_space=pl.ANY)] * 6,
        out_specs=(vmem, vmem, vmem),
        scratch_shapes=scratch,
        compiler_params=pltpu.CompilerParams(
            collective_id=0, has_side_effects=True, vmem_limit_bytes=63 * 2**20
        ),
    )(video, measured, mult_tv, mult_fit, counts, ranking.reshape(1, columns))


def solution(mesh):
    placed = (
        P(("grp", "dev"), None, None),
        P(("grp", "dev"), None, None),
        P(None, ("grp", "dev"), None, None),
        P(("grp", "dev"), None, None),
        P(("grp", "dev"), None),
        P(),
    )
    dev_count = mesh.shape["dev"]
    count = dev_count * mesh.shape["grp"]
    local = functools.partial(fused, dev_count, count) if count == CHUNKS else body
    return jax.shard_map(
        local,
        mesh=mesh,
        in_specs=placed,
        out_specs=(
            P(("grp", "dev"), None, None),
            P(None, ("grp", "dev"), None, None),
            P(("grp", "dev"), None, None),
        ),
        check_vma=False,
    )
```

```python
import functools
import math

import jax
import jax.numpy as jnp
from jax import lax
from jax.experimental import pallas as pl
from jax.experimental.pallas import tpu as pltpu
from jax.sharding import PartitionSpec as P

penalty_tv = 0.5
penalty_fit = 1.0
step_size = 0.2


def swapped(value, axis, stride):
    mask = 2**stride
    pairs = [(source, source ^ mask) for source in range(lax.axis_size(axis))]
    return lax.ppermute(value, axis, pairs)


def passed_along(value, axis, steps):
    count = lax.axis_size(axis)
    pairs = [(source, (source + steps) % count) for source in range(count)]
    return lax.ppermute(value, axis, pairs)


def sign_table(size_n):
    left = lax.broadcasted_iota(jnp.int32, (size_n, size_n), 0)
    right = lax.broadcasted_iota(jnp.int32, (size_n, size_n), 1)
    common = jnp.bitwise_and(left, right)
    total = jnp.zeros((size_n, size_n), jnp.int32)
    for bit_index in range(max(size_n.bit_length(), 1)):
        total = total + jnp.bitwise_and(jnp.right_shift(common, bit_index), 1)
    return (1 - 2 * jnp.bitwise_and(total, 1)).astype(jnp.float32)


def pair_steps(field, axis_kind):
    count = lax.axis_size("dev") if axis_kind == "dev" else lax.axis_size("grp")
    for bit_index in range(count.bit_length() - 1):
        if axis_kind == "dev":
            partner = swapped(field, "dev", bit_index)
            my_bit = jnp.bitwise_and(jnp.right_shift(lax.axis_index("dev"), bit_index), 1)
        else:
            partner = swapped(field, "grp", bit_index)
            my_bit = jnp.bitwise_and(jnp.right_shift(lax.axis_index("grp"), bit_index), 1)
        field = jnp.where(my_bit == 1, partner - field, field + partner)
    return field


def time_local(field, table_t):
    return jnp.einsum("st,trc->src", table_t, field, precision=lax.Precision.HIGHEST)


def transform(field):
    frames, rows, columns = field.shape
    dev_count = lax.axis_size("dev")
    grp_count = lax.axis_size("grp")
    total_frames = frames * dev_count * grp_count
    scale = 1.0 / math.sqrt(total_frames * columns)
    table_w = sign_table(columns)
    mixed = jnp.dot(field.reshape(-1, columns), table_w, precision=lax.Precision.HIGHEST).reshape(
        field.shape
    )
    mixed = time_local(mixed, sign_table(frames))
    mixed = pair_steps(mixed, "dev")
    mixed = pair_steps(mixed, "grp")
    return mixed * scale


def gradient(field):
    after = passed_along(field[:1], ("grp", "dev"), -1)
    extended = jnp.concatenate([field[1:], after], axis=0)
    return jnp.stack(
        [extended - field, jnp.roll(field, -1, 1) - field, jnp.roll(field, -1, 2) - field]
    )


def adjoint_tv(tension):
    before = passed_along(tension[0, -1:], ("grp", "dev"), 1)
    previous = jnp.concatenate([before, tension[0, :-1]], axis=0)
    return (
        previous
        - tension[0]
        + jnp.roll(tension[1], 1, 1)
        - tension[1]
        + jnp.roll(tension[2], 1, 2)
        - tension[2]
    )


def body(video, measured, multiplier_tv, multiplier_fit, counts, ranking):
    mask = (ranking[None, None, :] < counts[:, :, None]).astype(jnp.float32)
    slopes = gradient(video)
    shifted = slopes - multiplier_tv / penalty_tv
    length = jnp.sqrt(jnp.sum(shifted * shifted, axis=0))
    shrunk = shifted * (
        jnp.maximum(length - 1.0 / penalty_tv, 0.0) / jnp.maximum(length, 1.0 / penalty_tv)
    )
    tension = penalty_tv * (slopes - shrunk) - multiplier_tv
    weighted = mask * (penalty_fit * (transform(video) - measured) - multiplier_fit)
    descent = adjoint_tv(tension) + transform(weighted)
    video_next = video - step_size * descent
    tv_next = multiplier_tv - penalty_tv * (gradient(video_next) - shrunk)
    fit_next = multiplier_fit - penalty_fit * mask * (transform(video_next) - measured)
    return (video_next, tv_next, fit_next)


LANES = 128
USED = 112
GROUPS = 4
ROW_GROUPS = 8
CHUNKS = GROUPS * ROW_GROUPS
MESH_ID = pl.DeviceIdType.MESH


def walsh(value):
    size = value.shape[0]
    tail = value.shape[1:]
    half = 1
    while half < size:
        pairs = value.reshape((size // (2 * half), 2, half) + tail)
        low, high = pairs[:, 0:1], pairs[:, 1:2]
        value = jnp.concatenate([low + high, low - high], axis=1).reshape((size,) + tail)
        half *= 2
    return value


def halves(value):
    high = value.astype(jnp.bfloat16)
    low = (value - high.astype(jnp.float32)).astype(jnp.bfloat16)
    return jnp.concatenate([high, low], axis=0)


def times_transposed(value, table):
    out = lax.dot_general(
        halves(value), table, (((1,), (1,)), ((), ())), preferred_element_type=jnp.float32
    )
    return out[: value.shape[0]] + out[value.shape[0] :]


def times(value, table):
    out = jnp.dot(halves(value), table, preferred_element_type=jnp.float32)
    return out[: value.shape[0]] + out[value.shape[0] :]


def kernel(
    dev_count, count, scale,
    video_in, measured_in, mult_tv_in, mult_fit_in, counts_in, ranking_in,
    video_next, tv_next, fit_next,
    video, measured, mult_tv, mult_fit, counts, ranking,
    select, signs, mat, part, tens, moved,
    s_v, s_q, s_u, s_t, s_e,
    r_v, r_q, r_u, r_t, r_e,
    h_v, h_t, h_u, weighted, known, keep,
    load_sem, send_sem, recv_sem, halo_send, halo_recv,
):
    rows, columns = video.shape[1], video.shape[2]
    span = rows // ROW_GROUPS
    me = lax.axis_index("grp") * dev_count + lax.axis_index("dev")
    after = lax.rem(me + 1, count)
    before = lax.rem(me + count - 1, count)

    def coords(index):
        return (index // dev_count, lax.rem(index, dev_count))

    loads = [
        pltpu.make_async_copy(source, target, load_sem.at[slot])
        for slot, (source, target) in enumerate(
            (
                (ranking_in, ranking),
                (counts_in, counts),
                (video_in, video),
                (mult_tv_in, mult_tv),
                (measured_in, measured),
                (mult_fit_in, mult_fit),
            )
        )
    ]
    for load in loads:
        load.start()

    barrier = pltpu.get_barrier_semaphore()

    def greet(step, carry):
        other = lax.rem(me + step, count)
        pl.semaphore_signal(barrier, inc=1, device_id=coords(other), device_id_type=MESH_ID)
        return carry

    lax.fori_loop(1, count, greet, 0)

    def halo(slot, source, target, other):
        copy = pltpu.make_async_remote_copy(
            src_ref=source, dst_ref=target, send_sem=halo_send.at[slot],
            recv_sem=halo_recv.at[slot], device_id=coords(other), device_id_type=MESH_ID,
        )
        copy.start()
        return copy

    def spread(slot, source, target, frame=None):
        def step_to(step, carry):
            other = lax.rem(me + step, count)
            pltpu.make_async_remote_copy(
                src_ref=source(other),
                dst_ref=target.at[me] if frame is None else target.at[me, frame],
                send_sem=send_sem.at[slot],
                recv_sem=recv_sem.at[slot], device_id=coords(other), device_id_type=MESH_ID,
            ).start()
            return carry

        lax.fori_loop(1, count, step_to, 0)

    def arrived(slot, target, frame=None):
        held = target.at[pl.ds(0, count - 1)] if frame is None else target.at[pl.ds(0, count - 1), frame]
        pltpu.make_async_copy(held, held, recv_sem.at[slot]).wait()

    def sent(slot, target, frame=None):
        held = target.at[pl.ds(0, count - 1)] if frame is None else target.at[pl.ds(0, count - 1), frame]
        pltpu.make_async_copy(held, held, send_sem.at[slot]).wait()

    def cut_frame(value, target, frame):
        mat[:rows] = value
        for chunk in range(CHUNKS):
            row, lane = chunk // GROUPS * span, chunk % GROUPS * LANES
            target[chunk, frame] = mat[row : row + span, lane : lane + LANES]

    def cut(value, target):
        mat[...] = value
        for chunk in range(CHUNKS):
            row, lane = chunk // GROUPS * span, chunk % GROUPS * LANES
            for frame in range(2):
                start = frame * rows + row
                target[chunk, frame] = mat[start : start + span, lane : lane + LANES]

    def paste(source, target, frames):
        for chunk in range(CHUNKS):
            row, lane = chunk // GROUPS * span, chunk % GROUPS * LANES
            for frame in range(frames):
                start = frame * rows + row
                target[start : start + span, lane : lane + LANES] = source[chunk, frame]

    pl.semaphore_wait(barrier, count - 1)
    piece = rows // 2
    pieces = [pl.ds(0, piece), pl.ds(piece, piece)]
    halo_v = [
        halo(n, video_in.at[0, cut_rows], h_v.at[cut_rows], before)
        for n, cut_rows in enumerate(pieces)
    ]

    loads[0].wait()
    wide = GROUPS * LANES
    place = lax.broadcasted_iota(jnp.int32, (wide, LANES), 0)
    inner = lax.rem(place, LANES)
    rank = jnp.where(inner < USED, place // LANES * USED + inner, -1)
    lane_index = lax.broadcasted_iota(jnp.int32, (wide, LANES), 1)
    picked = jnp.zeros((wide, LANES), jnp.int32)
    for tile in range(columns // LANES):
        cols = slice(tile * LANES, (tile + 1) * LANES)
        hit = ranking[:, cols] == rank
        select[:, cols] = jnp.where(hit, 1.0, 0.0).astype(jnp.bfloat16)
        picked = picked + jnp.where(hit, lane_index + tile * LANES, 0)
    column = jnp.sum(picked.astype(jnp.float32), axis=1, keepdims=True).astype(jnp.int32)
    common = jnp.bitwise_and(column, lane_index)
    for shift in (4, 2, 1):
        common = jnp.bitwise_xor(common, jnp.right_shift(common, shift))
    low_sign = (1 - 2 * jnp.bitwise_and(common, 1)).astype(jnp.float32)
    for tile in range(columns // LANES):
        high = jnp.bitwise_and(jnp.right_shift(column, LANES.bit_length() - 1), tile)
        for shift in (4, 2, 1):
            high = jnp.bitwise_xor(high, jnp.right_shift(high, shift))
        sign = (1 - 2 * jnp.bitwise_and(high, 1)).astype(jnp.float32)
        signs[:, tile * LANES : (tile + 1) * LANES] = (low_sign * sign).astype(jnp.bfloat16)

    flat = (2 * rows, columns)
    loads[2].wait()
    cut(times_transposed(video[...].reshape(flat), signs[...]), s_v)
    spread(0, lambda other: s_v.at[other], r_v)
    r_v[me] = s_v[me]

    for load in (loads[1], loads[4], loads[5]):
        load.wait()
    square = (rows, rows)
    diagonal = lax.broadcasted_iota(jnp.int32, square, 0) == lax.broadcasted_iota(
        jnp.int32, square, 1
    )
    kept = []
    for frame in range(2):
        line = counts[frame : frame + 1, :].astype(jnp.float32)
        kept.append(jnp.sum(jnp.where(diagonal, line, 0.0), axis=1, keepdims=True))
    kept = jnp.concatenate(kept, axis=0)
    wanted = times_transposed((measured[...] + mult_fit[...]).reshape(flat), select[...])
    spare = lax.rem(lax.broadcasted_iota(jnp.int32, wanted.shape, 1), LANES) >= USED
    cut(jnp.where(spare, kept, wanted), s_q)

    loads[3].wait()

    def shrink(frame, where, ahead, down, right):
        here = video[frame, where]
        slopes = (ahead - here, down - here, right - here)
        mult = [mult_tv[k, frame, where] for k in range(3)]
        shifted = [slopes[k] - mult[k] / penalty_tv for k in range(3)]
        length = jnp.sqrt(
            shifted[0] * shifted[0] + shifted[1] * shifted[1] + shifted[2] * shifted[2]
        )
        edge = 1.0 / penalty_tv
        factor = jnp.maximum(length - edge, 0.0) / jnp.maximum(length, edge)
        for k in range(3):
            shrunk = shifted[k] * factor
            tens[k, frame, where] = penalty_tv * (slopes[k] - shrunk) - mult[k]
            part[k, frame, where] = mult[k] + penalty_tv * shrunk

    def rolled(frame):
        here = video[frame]
        return pltpu.roll(here, rows - 1, 0), pltpu.roll(here, columns - 1, 1)

    shrink(0, pl.ds(0, rows), video[1], *rolled(0))
    down, right = rolled(1)
    halo_t = []
    for n, where in enumerate(pieces):
        halo_v[n].wait()
        span_rows = slice(n * piece, (n + 1) * piece)
        shrink(1, where, h_v[where], down[span_rows], right[span_rows])
        halo_t.append(halo(2 + n, tens.at[0, 1, where], h_t.at[where], after))
    spread(1, lambda other: s_q.at[other], r_q)
    r_q[me] = s_q[me]

    def stepped(frame, previous):
        adjoint = (
            previous
            - tens[0, frame]
            + pltpu.roll(tens[1, frame], 1, 0)
            - tens[1, frame]
            + pltpu.roll(tens[2, frame], 1, 1)
            - tens[2, frame]
        )
        result = video[frame] - step_size * adjoint
        moved[frame] = result
        cut_frame(times_transposed(result, signs[...]), s_u, frame)
        spread(3 + frame, lambda other: s_u.at[other, frame], r_u, frame)
        r_u[me, frame] = s_u[me, frame]

    stepped(1, tens[0, 0])
    mask = ranking[...].astype(jnp.float32) < kept
    known[...] = mult_fit[...].reshape(flat) + jnp.where(mask, measured[...].reshape(flat), 0.0)
    halo_t[0].wait()
    halo_t[1].wait()
    stepped(0, h_t[...])

    arrived(0, r_v)
    arrived(1, r_q)
    chunk_shape = (2 * count, span, LANES)
    spectrum = walsh(r_v[...].reshape(chunk_shape)) * scale
    wish = r_q[...].reshape(chunk_shape)
    lanes = lax.broadcasted_iota(jnp.int32, chunk_shape, 2)
    own_rank = (lax.rem(me, GROUPS) * USED + lanes).astype(jnp.float32)
    inside = jnp.logical_and(lanes < USED, own_rank < wish[:, :, LANES - 1 :])
    keep[...] = jnp.where(inside, 1.0, 0.0)
    fresh = jnp.where(inside, spectrum - wish, 0.0) * penalty_fit
    weighted[...] = fresh
    back = walsh(fresh) * (scale * step_size)
    s_t[...] = back.reshape(s_t.shape)
    spread(2, lambda other: s_t.at[other], r_t)
    r_t[me] = s_t[me]

    arrived(3, r_u, 0)
    arrived(4, r_u, 1)
    spectrum = walsh(r_u[...].reshape(chunk_shape)) * scale
    left = keep[...] * penalty_fit * (spectrum - step_size * weighted[...])
    s_e[...] = left.reshape(s_e.shape)
    spread(5, lambda other: s_e.at[other], r_e)
    r_e[me] = s_e[me]

    arrived(2, r_t)
    paste(r_t, mat, 2)
    change = times(mat[...], signs[...])
    first = moved[0] - change[:rows]
    second = moved[1] - change[rows:]
    moved[0] = first
    halo_u = halo(4, moved.at[0], h_u, before)
    video_next[0] = first
    video_next[1] = second
    for frame, here in ((0, first), (1, second)):
        tv_next[1, frame] = part[1, frame] - penalty_tv * (pltpu.roll(here, rows - 1, 0) - here)
        tv_next[2, frame] = part[2, frame] - penalty_tv * (pltpu.roll(here, columns - 1, 1) - here)
    tv_next[0, 0] = part[0, 0] - penalty_tv * (second - first)
    arrived(5, r_e)
    paste(r_e, mat, 2)
    fit_next[...] = (known[...] - times(mat[...], select[...])).reshape(fit_next.shape)

    halo_u.wait()
    tv_next[0, 1] = part[0, 1] - penalty_tv * (h_u[...] - video_next[1])
    sent(0, r_v)
    sent(1, r_q)
    sent(2, r_t)
    sent(3, r_u, 0)
    sent(4, r_u, 1)
    sent(5, r_e)


def place(*refs):
    sources, targets, stages = refs[:3], refs[3:6], refs[6:9]
    in_sem, out_sem = refs[9:]
    loads, stores = [], []
    for source, target, stage in zip(sources, targets, stages):
        for n in range(source.shape[0]):
            slot = len(loads)
            loads.append(pltpu.make_async_copy(source.at[n], stage.at[n], in_sem.at[slot]))
            stores.append(pltpu.make_async_copy(stage.at[n], target.at[n], out_sem.at[slot]))
    for load in loads:
        load.start()
    for load, store in zip(loads, stores):
        load.wait()
        store.start()
    for store in stores:
        store.wait()


def fused(dev_count, count, video, measured, mult_tv, mult_fit, counts, ranking):
    frames, rows, columns = video.shape
    span = rows // ROW_GROUPS
    wide = GROUPS * LANES
    f32 = jnp.float32
    block = pltpu.VMEM((count, frames, span, LANES), f32)
    scratch = [
        pltpu.VMEM(video.shape, f32),
        pltpu.VMEM(video.shape, f32),
        pltpu.VMEM(mult_tv.shape, f32),
        pltpu.VMEM(video.shape, f32),
        pltpu.VMEM(counts.shape, jnp.int32),
        pltpu.VMEM((1, columns), jnp.int32),
        pltpu.VMEM((wide, columns), jnp.bfloat16),
        pltpu.VMEM((wide, columns), jnp.bfloat16),
        pltpu.VMEM((frames * rows, wide), f32),
        pltpu.VMEM(mult_tv.shape, f32),
        pltpu.VMEM(mult_tv.shape, f32),
        pltpu.VMEM(video.shape, f32),
        block, block, block, block, block,
        block, block, block, block, block,
        pltpu.VMEM((rows, columns), f32),
        pltpu.VMEM((rows, columns), f32),
        pltpu.VMEM((rows, columns), f32),
        pltpu.VMEM((frames * count, span, LANES), f32),
        pltpu.VMEM((frames * rows, columns), f32),
        pltpu.VMEM((frames * count, span, LANES), f32),
        pltpu.SemaphoreType.DMA((6,)),
        pltpu.SemaphoreType.DMA((6,)),
        pltpu.SemaphoreType.DMA((6,)),
        pltpu.SemaphoreType.DMA((5,)),
        pltpu.SemaphoreType.DMA((5,)),
    ]
    scale = 1.0 / math.sqrt(frames * count * columns)
    vmem = pl.BlockSpec(memory_space=pltpu.VMEM)
    shapes = (
        jax.ShapeDtypeStruct(video.shape, f32),
        jax.ShapeDtypeStruct(mult_tv.shape, f32),
        jax.ShapeDtypeStruct(video.shape, f32),
    )
    results = pl.pallas_call(
        functools.partial(kernel, dev_count, count, scale),
        out_shape=shapes,
        in_specs=[pl.BlockSpec(memory_space=pl.ANY)] * 6,
        out_specs=(vmem, vmem, vmem),
        scratch_shapes=scratch,
        compiler_params=pltpu.CompilerParams(
            collective_id=0, has_side_effects=True, vmem_limit_bytes=63 * 2**20
        ),
    )(video, measured, mult_tv, mult_fit, counts, ranking.reshape(1, columns))
    anywhere = pl.BlockSpec(memory_space=pl.ANY)
    return pl.pallas_call(
        place,
        out_shape=shapes,
        in_specs=[anywhere] * 3,
        out_specs=(anywhere,) * 3,
        scratch_shapes=[pltpu.VMEM(shape.shape, f32) for shape in shapes]
        + [pltpu.SemaphoreType.DMA((7,)), pltpu.SemaphoreType.DMA((7,))],
        compiler_params=pltpu.CompilerParams(vmem_limit_bytes=60 * 2**20),
    )(*results)


def solution(mesh):
    placed = (
        P(("grp", "dev"), None, None),
        P(("grp", "dev"), None, None),
        P(None, ("grp", "dev"), None, None),
        P(("grp", "dev"), None, None),
        P(("grp", "dev"), None),
        P(),
    )
    dev_count = mesh.shape["dev"]
    count = dev_count * mesh.shape["grp"]
    local = functools.partial(fused, dev_count, count) if count == CHUNKS else body
    return jax.shard_map(
        local,
        mesh=mesh,
        in_specs=placed,
        out_specs=(
            P(("grp", "dev"), None, None),
            P(None, ("grp", "dev"), None, None),
            P(("grp", "dev"), None, None),
        ),
        check_vma=False,
    )
```

```python
import functools
import math

import jax
import jax.numpy as jnp
from jax import lax
from jax.experimental import pallas as pl
from jax.experimental.pallas import tpu as pltpu
from jax.sharding import PartitionSpec as P

penalty_tv = 0.5
penalty_fit = 1.0
step_size = 0.2


def swapped(value, axis, stride):
    mask = 2**stride
    pairs = [(source, source ^ mask) for source in range(lax.axis_size(axis))]
    return lax.ppermute(value, axis, pairs)


def passed_along(value, axis, steps):
    count = lax.axis_size(axis)
    pairs = [(source, (source + steps) % count) for source in range(count)]
    return lax.ppermute(value, axis, pairs)


def sign_table(size_n):
    left = lax.broadcasted_iota(jnp.int32, (size_n, size_n), 0)
    right = lax.broadcasted_iota(jnp.int32, (size_n, size_n), 1)
    common = jnp.bitwise_and(left, right)
    total = jnp.zeros((size_n, size_n), jnp.int32)
    for bit_index in range(max(size_n.bit_length(), 1)):
        total = total + jnp.bitwise_and(jnp.right_shift(common, bit_index), 1)
    return (1 - 2 * jnp.bitwise_and(total, 1)).astype(jnp.float32)


def pair_steps(field, axis_kind):
    count = lax.axis_size("dev") if axis_kind == "dev" else lax.axis_size("grp")
    for bit_index in range(count.bit_length() - 1):
        if axis_kind == "dev":
            partner = swapped(field, "dev", bit_index)
            my_bit = jnp.bitwise_and(jnp.right_shift(lax.axis_index("dev"), bit_index), 1)
        else:
            partner = swapped(field, "grp", bit_index)
            my_bit = jnp.bitwise_and(jnp.right_shift(lax.axis_index("grp"), bit_index), 1)
        field = jnp.where(my_bit == 1, partner - field, field + partner)
    return field


def time_local(field, table_t):
    return jnp.einsum("st,trc->src", table_t, field, precision=lax.Precision.HIGHEST)


def transform(field):
    frames, rows, columns = field.shape
    dev_count = lax.axis_size("dev")
    grp_count = lax.axis_size("grp")
    total_frames = frames * dev_count * grp_count
    scale = 1.0 / math.sqrt(total_frames * columns)
    table_w = sign_table(columns)
    mixed = jnp.dot(field.reshape(-1, columns), table_w, precision=lax.Precision.HIGHEST).reshape(
        field.shape
    )
    mixed = time_local(mixed, sign_table(frames))
    mixed = pair_steps(mixed, "dev")
    mixed = pair_steps(mixed, "grp")
    return mixed * scale


def gradient(field):
    after = passed_along(field[:1], ("grp", "dev"), -1)
    extended = jnp.concatenate([field[1:], after], axis=0)
    return jnp.stack(
        [extended - field, jnp.roll(field, -1, 1) - field, jnp.roll(field, -1, 2) - field]
    )


def adjoint_tv(tension):
    before = passed_along(tension[0, -1:], ("grp", "dev"), 1)
    previous = jnp.concatenate([before, tension[0, :-1]], axis=0)
    return (
        previous
        - tension[0]
        + jnp.roll(tension[1], 1, 1)
        - tension[1]
        + jnp.roll(tension[2], 1, 2)
        - tension[2]
    )


def body(video, measured, multiplier_tv, multiplier_fit, counts, ranking):
    mask = (ranking[None, None, :] < counts[:, :, None]).astype(jnp.float32)
    slopes = gradient(video)
    shifted = slopes - multiplier_tv / penalty_tv
    length = jnp.sqrt(jnp.sum(shifted * shifted, axis=0))
    shrunk = shifted * (
        jnp.maximum(length - 1.0 / penalty_tv, 0.0) / jnp.maximum(length, 1.0 / penalty_tv)
    )
    tension = penalty_tv * (slopes - shrunk) - multiplier_tv
    weighted = mask * (penalty_fit * (transform(video) - measured) - multiplier_fit)
    descent = adjoint_tv(tension) + transform(weighted)
    video_next = video - step_size * descent
    tv_next = multiplier_tv - penalty_tv * (gradient(video_next) - shrunk)
    fit_next = multiplier_fit - penalty_fit * mask * (transform(video_next) - measured)
    return (video_next, tv_next, fit_next)


LANES = 128
USED = 112
GROUPS = 4
ROW_GROUPS = 8
CHUNKS = GROUPS * ROW_GROUPS
MESH_ID = pl.DeviceIdType.MESH


def walsh(value):
    size = value.shape[0]
    tail = value.shape[1:]
    half = 1
    while half < size:
        pairs = value.reshape((size // (2 * half), 2, half) + tail)
        low, high = pairs[:, 0:1], pairs[:, 1:2]
        value = jnp.concatenate([low + high, low - high], axis=1).reshape((size,) + tail)
        half *= 2
    return value


def halves(value):
    high = value.astype(jnp.bfloat16)
    low = (value - high.astype(jnp.float32)).astype(jnp.bfloat16)
    return jnp.concatenate([high, low], axis=0)


def times_transposed(value, table):
    out = lax.dot_general(
        halves(value), table, (((1,), (1,)), ((), ())), preferred_element_type=jnp.float32
    )
    return out[: value.shape[0]] + out[value.shape[0] :]


def times(value, table):
    out = jnp.dot(halves(value), table, preferred_element_type=jnp.float32)
    return out[: value.shape[0]] + out[value.shape[0] :]


def kernel(
    dev_count, count, scale,
    video_in, measured_in, mult_tv_in, mult_fit_in, counts_in, ranking_in,
    video_next, tv_next, fit_next,
    video, measured, mult_tv, mult_fit, counts, ranking,
    select, signs, mat, part, tens, moved,
    s_v, s_q, s_u, s_t, s_e,
    r_v, r_q, r_u, r_t, r_e,
    h_v, h_t, h_u, weighted, known, keep,
    load_sem, send_sem, recv_sem, halo_send, halo_recv,
):
    rows, columns = video.shape[1], video.shape[2]
    span = rows // ROW_GROUPS
    me = lax.axis_index("grp") * dev_count + lax.axis_index("dev")
    after = lax.rem(me + 1, count)
    before = lax.rem(me + count - 1, count)

    def coords(index):
        return (index // dev_count, lax.rem(index, dev_count))

    loads = [
        pltpu.make_async_copy(source, target, load_sem.at[slot])
        for slot, (source, target) in enumerate(
            (
                (ranking_in, ranking),
                (counts_in, counts),
                (video_in, video),
                (mult_tv_in, mult_tv),
                (measured_in, measured),
                (mult_fit_in, mult_fit),
            )
        )
    ]
    for load in loads:
        load.start()

    barrier = pltpu.get_barrier_semaphore()

    def greet(step, carry):
        other = lax.rem(me + step, count)
        pl.semaphore_signal(barrier, inc=1, device_id=coords(other), device_id_type=MESH_ID)
        return carry

    lax.fori_loop(1, count, greet, 0)

    def halo(slot, source, target, other):
        copy = pltpu.make_async_remote_copy(
            src_ref=source, dst_ref=target, send_sem=halo_send.at[slot],
            recv_sem=halo_recv.at[slot], device_id=coords(other), device_id_type=MESH_ID,
        )
        copy.start()
        return copy

    def spread(slot, source, target, frame=None):
        def step_to(step, carry):
            other = lax.rem(me + step, count)
            pltpu.make_async_remote_copy(
                src_ref=source(other),
                dst_ref=target.at[me] if frame is None else target.at[me, frame],
                send_sem=send_sem.at[slot],
                recv_sem=recv_sem.at[slot], device_id=coords(other), device_id_type=MESH_ID,
            ).start()
            return carry

        lax.fori_loop(1, count, step_to, 0)

    def arrived(slot, target, frame=None):
        held = target.at[pl.ds(0, count - 1)] if frame is None else target.at[pl.ds(0, count - 1), frame]
        pltpu.make_async_copy(held, held, recv_sem.at[slot]).wait()

    def sent(slot, target, frame=None):
        held = target.at[pl.ds(0, count - 1)] if frame is None else target.at[pl.ds(0, count - 1), frame]
        pltpu.make_async_copy(held, held, send_sem.at[slot]).wait()

    def cut_frame(value, target, frame):
        mat[:rows] = value
        for chunk in range(CHUNKS):
            row, lane = chunk // GROUPS * span, chunk % GROUPS * LANES
            target[chunk, frame] = mat[row : row + span, lane : lane + LANES]

    def cut(value, target):
        mat[...] = value
        for chunk in range(CHUNKS):
            row, lane = chunk // GROUPS * span, chunk % GROUPS * LANES
            for frame in range(2):
                start = frame * rows + row
                target[chunk, frame] = mat[start : start + span, lane : lane + LANES]

    def paste(source, target, frames):
        for chunk in range(CHUNKS):
            row, lane = chunk // GROUPS * span, chunk % GROUPS * LANES
            for frame in range(frames):
                start = frame * rows + row
                target[start : start + span, lane : lane + LANES] = source[chunk, frame]

    pl.semaphore_wait(barrier, count - 1)
    piece = rows // 2
    pieces = [pl.ds(0, piece), pl.ds(piece, piece)]
    halo_v = [
        halo(n, video_in.at[0, cut_rows], h_v.at[cut_rows], before)
        for n, cut_rows in enumerate(pieces)
    ]

    loads[0].wait()
    wide = GROUPS * LANES
    place = lax.broadcasted_iota(jnp.int32, (wide, LANES), 0)
    inner = lax.rem(place, LANES)
    rank = jnp.where(inner < USED, place // LANES * USED + inner, -1)
    lane_index = lax.broadcasted_iota(jnp.int32, (wide, LANES), 1)
    picked = jnp.zeros((wide, LANES), jnp.int32)
    for tile in range(columns // LANES):
        cols = slice(tile * LANES, (tile + 1) * LANES)
        hit = ranking[:, cols] == rank
        select[:, cols] = jnp.where(hit, 1.0, 0.0).astype(jnp.bfloat16)
        picked = picked + jnp.where(hit, lane_index + tile * LANES, 0)
    column = jnp.sum(picked.astype(jnp.float32), axis=1, keepdims=True).astype(jnp.int32)
    common = jnp.bitwise_and(column, lane_index)
    for shift in (4, 2, 1):
        common = jnp.bitwise_xor(common, jnp.right_shift(common, shift))
    low_sign = (1 - 2 * jnp.bitwise_and(common, 1)).astype(jnp.float32)
    for tile in range(columns // LANES):
        high = jnp.bitwise_and(jnp.right_shift(column, LANES.bit_length() - 1), tile)
        for shift in (4, 2, 1):
            high = jnp.bitwise_xor(high, jnp.right_shift(high, shift))
        sign = (1 - 2 * jnp.bitwise_and(high, 1)).astype(jnp.float32)
        signs[:, tile * LANES : (tile + 1) * LANES] = (low_sign * sign).astype(jnp.bfloat16)

    flat = (2 * rows, columns)
    loads[2].wait()
    cut(times_transposed(video[...].reshape(flat), signs[...]), s_v)
    spread(0, lambda other: s_v.at[other], r_v)
    r_v[me] = s_v[me]

    for load in (loads[1], loads[4], loads[5]):
        load.wait()
    square = (rows, rows)
    diagonal = lax.broadcasted_iota(jnp.int32, square, 0) == lax.broadcasted_iota(
        jnp.int32, square, 1
    )
    kept = []
    for frame in range(2):
        line = counts[frame : frame + 1, :].astype(jnp.float32)
        kept.append(jnp.sum(jnp.where(diagonal, line, 0.0), axis=1, keepdims=True))
    kept = jnp.concatenate(kept, axis=0)
    wanted = times_transposed((measured[...] + mult_fit[...]).reshape(flat), select[...])
    spare = lax.rem(lax.broadcasted_iota(jnp.int32, wanted.shape, 1), LANES) >= USED
    cut(jnp.where(spare, kept, wanted), s_q)

    loads[3].wait()

    def shrink(frame, where, ahead, down, right):
        here = video[frame, where]
        slopes = (ahead - here, down - here, right - here)
        mult = [mult_tv[k, frame, where] for k in range(3)]
        shifted = [slopes[k] - mult[k] / penalty_tv for k in range(3)]
        length = jnp.sqrt(
            shifted[0] * shifted[0] + shifted[1] * shifted[1] + shifted[2] * shifted[2]
        )
        edge = 1.0 / penalty_tv
        factor = jnp.maximum(length - edge, 0.0) / jnp.maximum(length, edge)
        for k in range(3):
            shrunk = shifted[k] * factor
            tens[k, frame, where] = penalty_tv * (slopes[k] - shrunk) - mult[k]
            part[k, frame, where] = mult[k] + penalty_tv * shrunk

    def rolled(frame):
        here = video[frame]
        return pltpu.roll(here, rows - 1, 0), pltpu.roll(here, columns - 1, 1)

    shrink(0, pl.ds(0, rows), video[1], *rolled(0))
    down, right = rolled(1)
    halo_t = []
    for n, where in enumerate(pieces):
        halo_v[n].wait()
        span_rows = slice(n * piece, (n + 1) * piece)
        shrink(1, where, h_v[where], down[span_rows], right[span_rows])
        halo_t.append(halo(2 + n, tens.at[0, 1, where], h_t.at[where], after))
    spread(1, lambda other: s_q.at[other], r_q)
    r_q[me] = s_q[me]

    def stepped(frame, previous):
        adjoint = (
            previous
            - tens[0, frame]
            + pltpu.roll(tens[1, frame], 1, 0)
            - tens[1, frame]
            + pltpu.roll(tens[2, frame], 1, 1)
            - tens[2, frame]
        )
        result = video[frame] - step_size * adjoint
        moved[frame] = result
        cut_frame(times_transposed(result, signs[...]), s_u, frame)
        spread(3 + frame, lambda other: s_u.at[other, frame], r_u, frame)
        r_u[me, frame] = s_u[me, frame]

    stepped(1, tens[0, 0])
    mask = ranking[...].astype(jnp.float32) < kept
    known[...] = mult_fit[...].reshape(flat) + jnp.where(mask, measured[...].reshape(flat), 0.0)
    halo_t[0].wait()
    halo_t[1].wait()
    stepped(0, h_t[...])

    arrived(0, r_v)
    arrived(1, r_q)
    chunk_shape = (2 * count, span, LANES)
    spectrum = walsh(r_v[...].reshape(chunk_shape)) * scale
    wish = r_q[...].reshape(chunk_shape)
    lanes = lax.broadcasted_iota(jnp.int32, chunk_shape, 2)
    own_rank = (lax.rem(me, GROUPS) * USED + lanes).astype(jnp.float32)
    inside = jnp.logical_and(lanes < USED, own_rank < wish[:, :, LANES - 1 :])
    keep[...] = jnp.where(inside, 1.0, 0.0)
    fresh = jnp.where(inside, spectrum - wish, 0.0) * penalty_fit
    weighted[...] = fresh
    back = walsh(fresh) * (scale * step_size)
    s_t[...] = back.reshape(s_t.shape)
    spread(2, lambda other: s_t.at[other], r_t)
    r_t[me] = s_t[me]

    arrived(3, r_u, 0)
    arrived(4, r_u, 1)
    spectrum = walsh(r_u[...].reshape(chunk_shape)) * scale
    left = keep[...] * penalty_fit * (spectrum - step_size * weighted[...])
    s_e[...] = left.reshape(s_e.shape)
    spread(5, lambda other: s_e.at[other], r_e)
    r_e[me] = s_e[me]

    arrived(2, r_t)
    paste(r_t, mat, 2)
    first = moved[0] - times(mat[:rows], signs[...])
    moved[0] = first
    halo_u = halo(4, moved.at[0], h_u, before)
    second = moved[1] - times(mat[rows:], signs[...])
    video_next[0] = first
    video_next[1] = second
    for frame, here in ((0, first), (1, second)):
        tv_next[1, frame] = part[1, frame] - penalty_tv * (pltpu.roll(here, rows - 1, 0) - here)
        tv_next[2, frame] = part[2, frame] - penalty_tv * (pltpu.roll(here, columns - 1, 1) - here)
    tv_next[0, 0] = part[0, 0] - penalty_tv * (second - first)
    arrived(5, r_e)
    paste(r_e, mat, 2)
    fit_next[...] = (known[...] - times(mat[...], select[...])).reshape(fit_next.shape)

    halo_u.wait()
    tv_next[0, 1] = part[0, 1] - penalty_tv * (h_u[...] - video_next[1])
    sent(0, r_v)
    sent(1, r_q)
    sent(2, r_t)
    sent(3, r_u, 0)
    sent(4, r_u, 1)
    sent(5, r_e)


def place(*refs):
    sources, targets, stages = refs[:3], refs[3:6], refs[6:9]
    in_sem, out_sem = refs[9:]
    loads, stores = [], []
    for source, target, stage in zip(sources, targets, stages):
        for n in range(source.shape[0]):
            slot = len(loads)
            loads.append(pltpu.make_async_copy(source.at[n], stage.at[n], in_sem.at[slot]))
            stores.append(pltpu.make_async_copy(stage.at[n], target.at[n], out_sem.at[slot]))
    for load in loads:
        load.start()
    for load, store in zip(loads, stores):
        load.wait()
        store.start()
    for store in stores:
        store.wait()


def fused(dev_count, count, video, measured, mult_tv, mult_fit, counts, ranking):
    frames, rows, columns = video.shape
    span = rows // ROW_GROUPS
    wide = GROUPS * LANES
    f32 = jnp.float32
    block = pltpu.VMEM((count, frames, span, LANES), f32)
    scratch = [
        pltpu.VMEM(video.shape, f32),
        pltpu.VMEM(video.shape, f32),
        pltpu.VMEM(mult_tv.shape, f32),
        pltpu.VMEM(video.shape, f32),
        pltpu.VMEM(counts.shape, jnp.int32),
        pltpu.VMEM((1, columns), jnp.int32),
        pltpu.VMEM((wide, columns), jnp.bfloat16),
        pltpu.VMEM((wide, columns), jnp.bfloat16),
        pltpu.VMEM((frames * rows, wide), f32),
        pltpu.VMEM(mult_tv.shape, f32),
        pltpu.VMEM(mult_tv.shape, f32),
        pltpu.VMEM(video.shape, f32),
        block, block, block, block, block,
        block, block, block, block, block,
        pltpu.VMEM((rows, columns), f32),
        pltpu.VMEM((rows, columns), f32),
        pltpu.VMEM((rows, columns), f32),
        pltpu.VMEM((frames * count, span, LANES), f32),
        pltpu.VMEM((frames * rows, columns), f32),
        pltpu.VMEM((frames * count, span, LANES), f32),
        pltpu.SemaphoreType.DMA((6,)),
        pltpu.SemaphoreType.DMA((6,)),
        pltpu.SemaphoreType.DMA((6,)),
        pltpu.SemaphoreType.DMA((5,)),
        pltpu.SemaphoreType.DMA((5,)),
    ]
    scale = 1.0 / math.sqrt(frames * count * columns)
    vmem = pl.BlockSpec(memory_space=pltpu.VMEM)
    shapes = (
        jax.ShapeDtypeStruct(video.shape, f32),
        jax.ShapeDtypeStruct(mult_tv.shape, f32),
        jax.ShapeDtypeStruct(video.shape, f32),
    )
    results = pl.pallas_call(
        functools.partial(kernel, dev_count, count, scale),
        out_shape=shapes,
        in_specs=[pl.BlockSpec(memory_space=pl.ANY)] * 6,
        out_specs=(vmem, vmem, vmem),
        scratch_shapes=scratch,
        compiler_params=pltpu.CompilerParams(
            collective_id=0, has_side_effects=True, vmem_limit_bytes=63 * 2**20
        ),
    )(video, measured, mult_tv, mult_fit, counts, ranking.reshape(1, columns))
    anywhere = pl.BlockSpec(memory_space=pl.ANY)
    return pl.pallas_call(
        place,
        out_shape=shapes,
        in_specs=[anywhere] * 3,
        out_specs=(anywhere,) * 3,
        scratch_shapes=[pltpu.VMEM(shape.shape, f32) for shape in shapes]
        + [pltpu.SemaphoreType.DMA((7,)), pltpu.SemaphoreType.DMA((7,))],
        compiler_params=pltpu.CompilerParams(vmem_limit_bytes=60 * 2**20),
    )(*results)


def solution(mesh):
    placed = (
        P(("grp", "dev"), None, None),
        P(("grp", "dev"), None, None),
        P(None, ("grp", "dev"), None, None),
        P(("grp", "dev"), None, None),
        P(("grp", "dev"), None),
        P(),
    )
    dev_count = mesh.shape["dev"]
    count = dev_count * mesh.shape["grp"]
    local = functools.partial(fused, dev_count, count) if count == CHUNKS else body
    return jax.shard_map(
        local,
        mesh=mesh,
        in_specs=placed,
        out_specs=(
            P(("grp", "dev"), None, None),
            P(None, ("grp", "dev"), None, None),
            P(("grp", "dev"), None, None),
        ),
        check_vma=False,
    )
```
